32 devices in a mesh: sa: 4 (over z), sb: 4 (over y, core), sl: 2 (over x).
Axes of the slice: x: 2, y: 2, z: 4, core: 2. Of those that a mesh axis runs over, the one named last changes fastest.
Arguments:
- stem_cache: bfloat16 [32, 2, 128, 4096], P(('sa', 'sb', 'sl')), may hold values from -6 to 6
- subtree_cache: bfloat16 [32, 2, 4096, 512], P(('sa', 'sb', 'sl')), may hold values from -0.0625 to 0.0625
- final_gates: bfloat16 [2, 512, 512], replicated, may hold values from -0.03125 to 0.03125
- group_rows: int32 [32], replicated, may hold values from 0 to 7
Outputs:
- amplitudes: float32 [512, 1024], P(('sa', 'sb', 'sl'))
The draws below stay inside these ranges and needn't reach their ends.
All inputs are finite; a program needn't handle non-finite values.
Results may differ from the reference program's by a relative error of at most 0.0029.
Values may be sent and summed in bfloat16 or wider, within the bound.
A program may use at most 64 MiB of HBM per device.

```python
import jax
import jax.numpy as jnp
from jax import lax

K = 4096
N = 512
M = 128
RB = 16
G = 32
R = 512
SLICES = 32
N_SA = 4
N_SB = 4
N_SL = 2


def with_ends(values, stream_key, smallest, high):
    place = [jax.random.randint(jax.random.fold_in(stream_key, axis), (), 0, length) for axis, length in enumerate(values.shape)]
    longest = values.shape.index(max(values.shape))
    beside = place[:longest] + [(place[longest] + 1) % values.shape[longest]] + place[longest + 1:]
    return values.at[tuple(place)].set(smallest).at[tuple(beside)].set(high)


def level_of(own_key, shape, split, smallest, largest):
    loudness = 1.0
    for dim, parts in split:
        draws = jax.random.uniform(jax.random.fold_in(jax.random.fold_in(own_key, 6), dim), (parts,), jnp.float32, smallest / len(split), largest / len(split))
        loudness = loudness * jnp.repeat(jnp.exp(draws), shape[dim] // parts).reshape((-1,) + (1,) * (len(shape) - 1 - dim))
    return loudness


def centred(rng, dims, deviation, bound, split=(), kind=jnp.bfloat16):
    result = deviation * jax.random.normal(rng, dims, jnp.float32)
    if split:
        result = result * level_of(rng, dims, split, -0.22, 0.18)
    return jnp.clip(result, -bound, bound).astype(kind)


def setup_inputs(seed: int = 0) -> dict:
    splits = jax.random.split(jax.random.key(seed), 5)
    stem_cache = centred(splits[0], (SLICES, 2, M, K), 1.0, 6.0, ((0, 32),))
    subtree_cache = centred(splits[1], (SLICES, 2, K, N), (2 * K) ** -0.5, 0.0625, ((0, 32),))
    final_gates = centred(splits[2], (2, N, N), (2 * N * SLICES) ** -0.5, 0.03125)
    group_rows = with_ends(jax.random.randint(splits[3], (G,), 0, M // RB), jax.random.fold_in(splits[3], 1), 0, (M // RB) - 1).astype(jnp.int32)
    return dict(stem_cache=stem_cache, subtree_cache=subtree_cache, final_gates=final_gates, group_rows=group_rows)


def reference(stem_cache, subtree_cache, final_gates, group_rows):
    half = M // 2
    flip_a = (N_SA // 2) * N_SB * N_SL
    rows = jnp.arange(R, dtype=jnp.int32)
    source = (jnp.take(group_rows, rows // RB) * RB + rows % RB).astype(jnp.int32)

    def one_slice(index, total):
        lower = lax.dynamic_index_in_dim(stem_cache, index, 0, keepdims=False)
        other = lax.dynamic_index_in_dim(stem_cache, jnp.bitwise_xor(index, N_SL).astype(jnp.int32), 0, keepdims=False)
        stem = jnp.concatenate([lower[:, :half], other[:, half:]], axis=1)
        sub = lax.dynamic_index_in_dim(subtree_cache, jnp.bitwise_xor(index, flip_a).astype(jnp.int32), 0, keepdims=False)
        real = jnp.dot(stem[0], sub[0], preferred_element_type=jnp.float32) - jnp.dot(stem[1], sub[1], preferred_element_type=jnp.float32)
        imag = jnp.dot(stem[0], sub[1], preferred_element_type=jnp.float32) + jnp.dot(stem[1], sub[0], preferred_element_type=jnp.float32)
        partial_s = jnp.stack([real, imag]).astype(jnp.bfloat16)
        return total + jnp.take(partial_s, source, axis=1).astype(jnp.float32)

    summed = lax.fori_loop(0, SLICES, one_slice, jnp.zeros((2, R, N), jnp.float32))
    gates = final_gates.astype(jnp.float32)
    hp = lax.Precision.HIGHEST
    real = jnp.dot(summed[0], gates[0], precision=hp) - jnp.dot(summed[1], gates[1], precision=hp)
    imag = jnp.dot(summed[0], gates[1], precision=hp) + jnp.dot(summed[1], gates[0], precision=hp)
    return jnp.concatenate([real, imag], axis=1)
```

```python
import functools

import jax
import jax.numpy as jnp
from jax import lax
from jax.experimental import pallas as pl
from jax.experimental.pallas import tpu as pltpu
from jax.sharding import PartitionSpec as P

RB = 16
AXES = ("sa", "sb", "sl")
STAGE = 2 * RB
LANES = 128
MESH = pl.DeviceIdType.MESH


def kernel(n_sa, n_sb, n_sl, row_groups, stem, subtree, gates, group_rows, out, held, sub, gate, part, rs, zb, ag,
           sub_sem, gate_sem, stem_send, stem_recv, rs_send, rs_recv, z_send, z_recv, ag_send, ag_recv):
    sa, sb, sl = (lax.axis_index(a) for a in AXES)
    stages = held.shape[0]
    n = subtree.shape[2]
    owners = 4 * n_sb
    per_half = owners // 2
    me = (sa % 2) * (2 * n_sb) + sb * 2 + sl % 2
    others = (n_sa // 2) * (n_sl // 2)
    my_q = (sa // 2) * (n_sl // 2) + sl // 2

    def owner_device(o):
        return ((sa // 2) * 2 + o // (2 * n_sb), (o // 2) % n_sb, (sl // 2) * 2 + o % 2)

    def other_device(q):
        return ((q // (n_sl // 2)) * 2 + sa % 2, sb, (q % (n_sl // 2)) * 2 + sl % 2)

    far = lax.rem(sa + n_sa // 2, n_sa)
    pair = sb + 1 - 2 * (sb % 2)

    pltpu.make_async_copy(subtree, sub, sub_sem).start()
    pltpu.make_async_copy(gates, gate, gate_sem).start()

    barrier = pltpu.get_barrier_semaphore()
    for b in (sb, pair):
        pl.semaphore_signal(barrier, inc=1, device_id=(far, b, sl), device_id_type=MESH)

    @pl.loop(1, owners)
    def _(j):
        pl.semaphore_signal(barrier, inc=1, device_id=owner_device((me + j) % owners), device_id_type=MESH)

    @pl.loop(1, others)
    def _(j):
        pl.semaphore_signal(barrier, inc=1, device_id=other_device((my_q + j) % others), device_id_type=MESH)

    pl.semaphore_wait(barrier, 2 + (owners - 1) + (others - 1))

    def stem_copy(t):
        target = sb if t < stages // 2 else pair
        return pltpu.make_async_remote_copy(
            src_ref=stem.at[:, pl.ds(t * STAGE, STAGE), :], dst_ref=held.at[t], send_sem=stem_send.at[t],
            recv_sem=stem_recv.at[t], device_id=(far, target, sl), device_id_type=MESH)

    def rs_copy(t, to, slot):
        return pltpu.make_async_remote_copy(
            src_ref=part.at[t, to], dst_ref=rs.at[t, slot], send_sem=rs_send.at[t, to],
            recv_sem=rs_recv.at[t, slot], device_id=owner_device(to), device_id_type=MESH)

    def z_copy(t, to, slot):
        return pltpu.make_async_remote_copy(
            src_ref=zb.at[t, slot], dst_ref=zb.at[t, slot], send_sem=z_send.at[t, to],
            recv_sem=z_recv.at[t, slot], device_id=other_device(to), device_id_type=MESH)

    def ag_copy(t, to, slot):
        piece = ag.at[2 * t + slot // per_half, slot % per_half]
        return pltpu.make_async_remote_copy(
            src_ref=piece, dst_ref=piece, send_sem=ag_send.at[t, to],
            recv_sem=ag_recv.at[t, slot], device_id=owner_device(to), device_id_type=MESH)

    for t in range(stages):
        stem_copy(t).start()
    pltpu.make_async_copy(subtree, sub, sub_sem).wait()
    pltpu.make_async_copy(gates, gate, gate_sem).wait()

    for t in range(stages):
        stem_copy(t).wait_recv()

        @functools.partial(lax.fori_loop, 0, 2, init_val=0)
        def _(i, carry, t=t):
            cols = pl.ds(pl.multiple_of(i * (n // 2), n // 2), n // 2)
            left = held[t].reshape(2 * STAGE, held.shape[3])
            by_real = jnp.dot(left, sub[0, :, cols], preferred_element_type=jnp.float32)
            by_imag = jnp.dot(left, sub[1, :, cols], preferred_element_type=jnp.float32)
            real = (by_real[:STAGE] - by_imag[STAGE:]).astype(jnp.bfloat16)
            imag = (by_imag[:STAGE] + by_real[STAGE:]).astype(jnp.bfloat16)
            pieces = n // 2 // LANES
            for half in range(2):
                for p in range(pieces):
                    at = half * per_half + i * pieces + p
                    block = (slice(half * RB, (half + 1) * RB), slice(p * LANES, (p + 1) * LANES))
                    part[t, at] = real[block]
                    part[t, at + per_half // 2] = imag[block]
            return carry

        @pl.loop(1, owners)
        def _(j):
            rs_copy(t, (me + j) % owners, me).start()

        rs[t, me] = part[t, me]

        @pl.loop(1, owners)
        def _(j):
            rs_copy(t, (me + j) % owners, (me + j) % owners).wait_recv()

        zb[t, my_q] = jnp.sum(rs[t].astype(jnp.float32), axis=0)

        @pl.loop(1, others)
        def _(j):
            z_copy(t, (my_q + j) % others, my_q).start()

        @pl.loop(1, others)
        def _(j):
            z_copy(t, (my_q + j) % others, (my_q + j) % others).wait_recv()

        ag[2 * t + me // per_half, me % per_half] = jnp.sum(zb[t], axis=0)

        @pl.loop(1, owners)
        def _(j):
            ag_copy(t, (me + j) % owners, me).start()

    for t in range(stages):
        stem_copy(t).wait_send()

        @pl.loop(1, owners)
        def _(j):
            rs_copy(t, (me + j) % owners, me).wait_send()

        @pl.loop(1, others)
        def _(j):
            z_copy(t, (my_q + j) % others, my_q).wait_send()

        @pl.loop(1, owners)
        def _(j):
            ag_copy(t, (me + j) % owners, (me + j) % owners).wait_recv()

        @pl.loop(1, owners)
        def _(j):
            ag_copy(t, (me + j) % owners, me).wait_send()

    device = (sa * n_sb + sb) * n_sl + sl
    block = ag[group_rows[device // row_groups]]
    rows = jnp.concatenate([block[p] for p in range(per_half)], axis=1)
    high = rows.astype(jnp.bfloat16)
    rest = rows - high.astype(jnp.float32)
    middle = rest.astype(jnp.bfloat16)
    low = (rest - middle.astype(jnp.float32)).astype(jnp.bfloat16)
    thirds = jnp.concatenate([low, middle, high], axis=0)

    def times(k, g):
        x = jnp.dot(thirds[:, k * n:(k + 1) * n], gate[g], preferred_element_type=jnp.float32)
        return x[:RB] + x[RB:2 * RB] + x[2 * RB:]

    out[:, :n] = times(0, 0) - times(1, 1)
    out[:, n:] = times(0, 1) + times(1, 0)


def local(stem_cache, subtree_cache, final_gates, group_rows):
    stem, subtree = stem_cache[0], subtree_cache[0]
    n_sa, n_sb, n_sl = (lax.axis_size(a) for a in AXES)
    m, k = stem.shape[1:]
    n = subtree.shape[2]
    stages = m // STAGE
    owners = 4 * n_sb
    others = (n_sa // 2) * (n_sl // 2)
    count = n_sa * n_sb * n_sl
    out_rows = group_rows.shape[0] * RB // count
    dma = pltpu.SemaphoreType.DMA
    block = pl.pallas_call(
        functools.partial(kernel, n_sa, n_sb, n_sl, RB // out_rows),
        out_shape=jax.ShapeDtypeStruct((RB, 2 * n), jnp.float32),
        in_specs=[pl.BlockSpec(memory_space=pl.ANY)] * 3 + [pl.BlockSpec(memory_space=pltpu.SMEM)],
        out_specs=pl.BlockSpec(memory_space=pltpu.VMEM),
        scratch_shapes=[
            pltpu.VMEM((stages, 2, STAGE, k), jnp.bfloat16),
            pltpu.VMEM((2, k, n), jnp.bfloat16),
            pltpu.VMEM((2, n, n), jnp.bfloat16),
            pltpu.VMEM((stages, owners, RB, LANES), jnp.bfloat16),
            pltpu.VMEM((stages, owners, RB, LANES), jnp.bfloat16),
            pltpu.VMEM((stages, others, RB, LANES), jnp.float32),
            pltpu.VMEM((2 * stages, owners // 2, RB, LANES), jnp.float32),
            dma, dma, dma((stages,)), dma((stages,)),
            dma((stages, owners)), dma((stages, owners)),
            dma((stages, others)), dma((stages, others)),
            dma((stages, owners)), dma((stages, owners)),
        ],
        compiler_params=pltpu.CompilerParams(
            collective_id=0, has_side_effects=True, vmem_limit_bytes=40 * 1024 * 1024
        ),
    )(stem, subtree, final_gates, group_rows)
    if out_rows == RB:
        return block
    return lax.dynamic_slice_in_dim(block, lax.axis_index(AXES) * out_rows % RB, out_rows, axis=0)


def solution(mesh):
    return jax.shard_map(
        local,
        mesh=mesh,
        in_specs=(
            P(AXES, None, None, None),
            P(AXES, None, None, None),
            P(),
            P(),
        ),
        out_specs=P(AXES, None),
        check_vma=False,
    )
```

```python
import functools
import itertools

import jax
import jax.numpy as jnp
from jax import lax
from jax.experimental import pallas as pl
from jax.experimental.pallas import tpu as pltpu
from jax.sharding import PartitionSpec as P

RB = 16
AXES = ("sa", "sb", "sl")
STAGE = 2 * RB
LANES = 128
MESH = pl.DeviceIdType.MESH


def kernel(n_sa, n_sb, n_sl, row_groups, stem, subtree, gates, group_rows, out, held, sub, gate, part, rs, zb, ag,
           sub_sem, gate_sem, stem_send, stem_recv, rs_send, rs_recv, z_send, z_recv, ag_send, ag_recv):
    sa, sb, sl = (lax.axis_index(a) for a in AXES)
    stages = held.shape[0]
    n = subtree.shape[2]
    owners = 4 * n_sb
    per_half = owners // 2
    me = (sa % 2) * (2 * n_sb) + sb * 2 + sl % 2
    others = (n_sa // 2) * (n_sl // 2)
    my_q = (sa // 2) * (n_sl // 2) + sl // 2

    near_peers = []
    for da, db, dl in itertools.product((0, 1), range(n_sb), (0, 1)):
        if da or db or dl:
            a, b, l = (sa + da) % 2, (sb + db) % n_sb, (sl + dl) % 2
            near_peers.append((a * (2 * n_sb) + b * 2 + l, (sa - sa % 2 + a, b, sl - sl % 2 + l)))
    near_peers.reverse()
    far_peers = []
    for da, dl in itertools.product(range(n_sa // 2), range(n_sl // 2)):
        if da or dl:
            far_peers.append(((sa + 2 * da) % n_sa, sb, (sl + 2 * dl) % n_sl))

    far = lax.rem(sa + n_sa // 2, n_sa)
    pair = sb + 1 - 2 * (sb % 2)

    pltpu.make_async_copy(subtree, sub, sub_sem).start()
    pltpu.make_async_copy(gates, gate, gate_sem).start()

    barrier = pltpu.get_barrier_semaphore()
    for b in (sb, pair):
        pl.semaphore_signal(barrier, inc=1, device_id=(far, b, sl), device_id_type=MESH)

    for device in [d for _, d in near_peers] + far_peers:
        pl.semaphore_signal(barrier, inc=1, device_id=device, device_id_type=MESH)

    pl.semaphore_wait(barrier, 2 + (owners - 1) + (others - 1))

    def stem_copy(i):
        target = sb if i < stages else pair
        return pltpu.make_async_remote_copy(
            src_ref=stem.at[:, pl.ds(i * RB, RB), :], dst_ref=held.at[i // 2, :, pl.ds(i % 2 * RB, RB)],
            send_sem=stem_send.at[i], recv_sem=stem_recv.at[i], device_id=(far, target, sl), device_id_type=MESH)

    def rs_copy(t, peer):
        slot, device = peer
        return pltpu.make_async_remote_copy(
            src_ref=part.at[t, slot], dst_ref=rs.at[t, me], send_sem=rs_send.at[t],
            recv_sem=rs_recv.at[t], device_id=device, device_id_type=MESH)

    def z_copy(t, device):
        return pltpu.make_async_remote_copy(
            src_ref=zb.at[t, my_q], dst_ref=zb.at[t, my_q], send_sem=z_send.at[t],
            recv_sem=z_recv.at[t], device_id=device, device_id_type=MESH)

    def ag_copy(t, peer):
        piece = ag.at[t, me]
        return pltpu.make_async_remote_copy(
            src_ref=piece, dst_ref=piece, send_sem=ag_send.at[t],
            recv_sem=ag_recv.at[t], device_id=peer[1], device_id_type=MESH)

    def wait_all(buffer, t, count, sem):
        if count:
            block = buffer.at[t, pl.ds(0, count)]
            pltpu.make_async_copy(block, block, sem.at[t]).wait()

    for i in range(2):
        stem_copy(i).start()
    pltpu.make_async_copy(subtree, sub, sub_sem).wait()
    pltpu.make_async_copy(gates, gate, gate_sem).wait()

    for t in range(stages):
        for i in (2 * t, 2 * t + 1):
            stem_copy(i).wait_send()
            if i + 2 < 2 * stages:
                stem_copy(i + 2).start()
        for i in (2 * t, 2 * t + 1):
            stem_copy(i).wait_recv()

        @functools.partial(lax.fori_loop, 0, 2, init_val=0)
        def _(i, carry, t=t):
            cols = pl.ds(pl.multiple_of(i * (n // 2), n // 2), n // 2)
            left = held[t].reshape(2 * STAGE, held.shape[3])
            by_real = jnp.dot(left, sub[0, :, cols], preferred_element_type=jnp.float32)
            by_imag = jnp.dot(left, sub[1, :, cols], preferred_element_type=jnp.float32)
            real = (by_real[:STAGE] - by_imag[STAGE:]).astype(jnp.bfloat16)
            imag = (by_imag[:STAGE] + by_real[STAGE:]).astype(jnp.bfloat16)
            pieces = n // 2 // LANES
            for half in range(2):
                for p in range(pieces):
                    at = half * per_half + i * pieces + p
                    block = (slice(half * RB, (half + 1) * RB), slice(p * LANES, (p + 1) * LANES))
                    part[t, at] = real[block]
                    part[t, at + per_half // 2] = imag[block]
            return carry

        for peer in near_peers:
            rs_copy(t, peer).start()

        rs[t, me] = part[t, me]

        wait_all(rs, t, owners - 1, rs_recv)

        zb[t, my_q] = jnp.sum(rs[t].astype(jnp.float32), axis=0)

        for device in far_peers:
            z_copy(t, device).start()

        wait_all(zb, t, others - 1, z_recv)

        ag[t, me] = jnp.sum(zb[t], axis=0)

        for peer in near_peers:
            ag_copy(t, peer).start()

    for t in range(stages):

        wait_all(part, t, owners - 1, rs_send)

        wait_all(zb, t, others - 1, z_send)

        wait_all(ag, t, owners - 1, ag_recv)

        wait_all(ag, t, owners - 1, ag_send)

    device = (sa * n_sb + sb) * n_sl + sl
    group = group_rows[device // row_groups]
    block = ag[group // 2, pl.ds(group % 2 * per_half, per_half)]
    rows = jnp.concatenate([block[p] for p in range(per_half)], axis=1)
    high = rows.astype(jnp.bfloat16)
    rest = rows - high.astype(jnp.float32)
    middle = rest.astype(jnp.bfloat16)
    low = (rest - middle.astype(jnp.float32)).astype(jnp.bfloat16)
    thirds = jnp.concatenate([low, middle, high], axis=0)

    def times(k, g):
        x = jnp.dot(thirds[:, k * n:(k + 1) * n], gate[g], preferred_element_type=jnp.float32)
        return x[:RB] + x[RB:2 * RB] + x[2 * RB:]

    out[:, :n] = times(0, 0) - times(1, 1)
    out[:, n:] = times(0, 1) + times(1, 0)


def local(stem_cache, subtree_cache, final_gates, group_rows):
    stem, subtree = stem_cache[0], subtree_cache[0]
    n_sa, n_sb, n_sl = (lax.axis_size(a) for a in AXES)
    m, k = stem.shape[1:]
    n = subtree.shape[2]
    stages = m // STAGE
    owners = 4 * n_sb
    others = (n_sa // 2) * (n_sl // 2)
    count = n_sa * n_sb * n_sl
    out_rows = group_rows.shape[0] * RB // count
    dma = pltpu.SemaphoreType.DMA
    block = pl.pallas_call(
        functools.partial(kernel, n_sa, n_sb, n_sl, RB // out_rows),
        out_shape=jax.ShapeDtypeStruct((RB, 2 * n), jnp.float32),
        in_specs=[pl.BlockSpec(memory_space=pl.ANY)] * 3 + [pl.BlockSpec(memory_space=pltpu.SMEM)],
        out_specs=pl.BlockSpec(memory_space=pltpu.VMEM),
        scratch_shapes=[
            pltpu.VMEM((stages, 2, STAGE, k), jnp.bfloat16),
            pltpu.VMEM((2, k, n), jnp.bfloat16),
            pltpu.VMEM((2, n, n), jnp.bfloat16),
            pltpu.VMEM((stages, owners, RB, LANES), jnp.bfloat16),
            pltpu.VMEM((stages, owners, RB, LANES), jnp.bfloat16),
            pltpu.VMEM((stages, others, RB, LANES), jnp.float32),
            pltpu.VMEM((stages, owners, RB, LANES), jnp.float32),
            dma, dma, dma((2 * stages,)), dma((2 * stages,)),
            dma((stages,)), dma((stages,)), dma((stages,)), dma((stages,)), dma((stages,)), dma((stages,)),
        ],
        compiler_params=pltpu.CompilerParams(
            collective_id=0, has_side_effects=True, vmem_limit_bytes=60 * 1024 * 1024
        ),
    )(stem, subtree, final_gates, group_rows)
    if out_rows == RB:
        return block
    return lax.dynamic_slice_in_dim(block, lax.axis_index(AXES) * out_rows % RB, out_rows, axis=0)


def solution(mesh):
    return jax.shard_map(
        local,
        mesh=mesh,
        in_specs=(
            P(AXES, None, None, None),
            P(AXES, None, None, None),
            P(),
            P(),
        ),
        out_specs=P(AXES, None),
        check_vma=False,
    )
```

```python
import functools
import itertools

import jax
import jax.numpy as jnp
from jax import lax
from jax.experimental import pallas as pl
from jax.experimental.pallas import tpu as pltpu
from jax.sharding import PartitionSpec as P

RB = 16
AXES = ("sa", "sb", "sl")
STAGE = 2 * RB
LANES = 128
CUTS = 2
MESH = pl.DeviceIdType.MESH


def kernel(n_sa, n_sb, n_sl, row_groups, stem, subtree, gates, group_rows, out, held, sub, gate, total, part, rs, zb, ag,
           sub_sem, gate_sem, stem_send, stem_recv, rs_send, rs_recv, z_send, z_recv, ag_send, ag_recv):
    sa, sb, sl = (lax.axis_index(a) for a in AXES)
    stages = held.shape[0]
    depth = held.shape[3] // CUTS
    n = subtree.shape[2]
    owners = 4 * n_sb
    per_half = owners // 2
    me = (sa % 2) * (2 * n_sb) + sb * 2 + sl % 2
    others = (n_sa // 2) * (n_sl // 2)
    my_q = (sa // 2) * (n_sl // 2) + sl // 2

    near_peers = []
    for da, db, dl in itertools.product((0, 1), range(n_sb), (0, 1)):
        if da or db or dl:
            a, b, l = (sa + da) % 2, (sb + db) % n_sb, (sl + dl) % 2
            near_peers.append((a * (2 * n_sb) + b * 2 + l, (sa - sa % 2 + a, b, sl - sl % 2 + l)))
    near_peers.reverse()
    far_peers = []
    for da, dl in itertools.product(range(n_sa // 2), range(n_sl // 2)):
        if da or dl:
            far_peers.append(((sa + 2 * da) % n_sa, sb, (sl + 2 * dl) % n_sl))

    far = lax.rem(sa + n_sa // 2, n_sa)
    pair = sb + 1 - 2 * (sb % 2)

    pltpu.make_async_copy(subtree, sub, sub_sem).start()
    pltpu.make_async_copy(gates, gate, gate_sem).start()

    barrier = pltpu.get_barrier_semaphore()
    for b in (sb, pair):
        pl.semaphore_signal(barrier, inc=1, device_id=(far, b, sl), device_id_type=MESH)

    for device in [d for _, d in near_peers] + far_peers:
        pl.semaphore_signal(barrier, inc=1, device_id=device, device_id_type=MESH)

    pl.semaphore_wait(barrier, 2 + (owners - 1) + (others - 1))

    def stem_copy(i):
        t, cut = divmod(i, CUTS)
        target = sb if t < stages // 2 else pair
        return pltpu.make_async_remote_copy(
            src_ref=stem.at[:, pl.ds(t * STAGE, STAGE), pl.ds(cut * depth, depth)],
            dst_ref=held.at[t, :, :, pl.ds(cut * depth, depth)],
            send_sem=stem_send.at[i], recv_sem=stem_recv.at[i], device_id=(far, target, sl), device_id_type=MESH)

    def rs_copy(t, peer):
        slot, device = peer
        return pltpu.make_async_remote_copy(
            src_ref=part.at[t, slot], dst_ref=rs.at[t, me], send_sem=rs_send.at[t],
            recv_sem=rs_recv.at[t], device_id=device, device_id_type=MESH)

    def z_copy(t, device):
        return pltpu.make_async_remote_copy(
            src_ref=zb.at[t, my_q], dst_ref=zb.at[t, my_q], send_sem=z_send.at[t],
            recv_sem=z_recv.at[t], device_id=device, device_id_type=MESH)

    def ag_copy(t, peer):
        piece = ag.at[t, me]
        return pltpu.make_async_remote_copy(
            src_ref=piece, dst_ref=piece, send_sem=ag_send.at[t],
            recv_sem=ag_recv.at[t], device_id=peer[1], device_id_type=MESH)

    def wait_all(buffer, t, count, sem):
        if count:
            block = buffer.at[t, pl.ds(0, count)]
            pltpu.make_async_copy(block, block, sem.at[t]).wait()

    for i in range(2):
        stem_copy(i).start()
    pltpu.make_async_copy(subtree, sub, sub_sem).wait()
    pltpu.make_async_copy(gates, gate, gate_sem).wait()

    for t in range(stages):
        for cut in range(CUTS):
            i = t * CUTS + cut
            stem_copy(i).wait_send()
            if i + 2 < CUTS * stages:
                stem_copy(i + 2).start()
            stem_copy(i).wait_recv()
            deep = slice(cut * depth, (cut + 1) * depth)
            left = held[t, :, :, deep].reshape(2 * STAGE, depth)
            for g in range(2):
                product = jnp.dot(left, sub[g, deep, :], preferred_element_type=jnp.float32)
                if cut == 0:
                    total[g] = product
                else:
                    total[g] += product

        real = (total[0, :STAGE] - total[1, STAGE:]).astype(jnp.bfloat16)
        imag = (total[1, :STAGE] + total[0, STAGE:]).astype(jnp.bfloat16)
        for half in range(2):
            for p in range(per_half // 2):
                block = (slice(half * RB, (half + 1) * RB), slice(p * LANES, (p + 1) * LANES))
                part[t, half * per_half + p] = real[block]
                part[t, half * per_half + per_half // 2 + p] = imag[block]

        for peer in near_peers:
            rs_copy(t, peer).start()

        rs[t, me] = part[t, me]

        wait_all(rs, t, owners - 1, rs_recv)

        zb[t, my_q] = jnp.sum(rs[t].astype(jnp.float32), axis=0)

        for device in far_peers:
            z_copy(t, device).start()

        wait_all(zb, t, others - 1, z_recv)

        ag[t, me] = jnp.sum(zb[t], axis=0)

        for peer in near_peers:
            ag_copy(t, peer).start()

    for t in range(stages):

        wait_all(part, t, owners - 1, rs_send)

        wait_all(zb, t, others - 1, z_send)

        wait_all(ag, t, owners - 1, ag_recv)

        wait_all(ag, t, owners - 1, ag_send)

    device = (sa * n_sb + sb) * n_sl + sl
    group = group_rows[device // row_groups]
    block = ag[group // 2, pl.ds(group % 2 * per_half, per_half)]
    rows = jnp.concatenate([block[p] for p in range(per_half)], axis=1)
    high = rows.astype(jnp.bfloat16)
    rest = rows - high.astype(jnp.float32)
    middle = rest.astype(jnp.bfloat16)
    low = (rest - middle.astype(jnp.float32)).astype(jnp.bfloat16)
    thirds = jnp.concatenate([low, middle, high], axis=0)

    def times(k, g):
        x = jnp.dot(thirds[:, k * n:(k + 1) * n], gate[g], preferred_element_type=jnp.float32)
        return x[:RB] + x[RB:2 * RB] + x[2 * RB:]

    out[:, :n] = times(0, 0) - times(1, 1)
    out[:, n:] = times(0, 1) + times(1, 0)


def local(stem_cache, subtree_cache, final_gates, group_rows):
    stem, subtree = stem_cache[0], subtree_cache[0]
    n_sa, n_sb, n_sl = (lax.axis_size(a) for a in AXES)
    m, k = stem.shape[1:]
    n = subtree.shape[2]
    stages = m // STAGE
    owners = 4 * n_sb
    others = (n_sa // 2) * (n_sl // 2)
    count = n_sa * n_sb * n_sl
    out_rows = group_rows.shape[0] * RB // count
    dma = pltpu.SemaphoreType.DMA
    block = pl.pallas_call(
        functools.partial(kernel, n_sa, n_sb, n_sl, RB // out_rows),
        out_shape=jax.ShapeDtypeStruct((RB, 2 * n), jnp.float32),
        in_specs=[pl.BlockSpec(memory_space=pl.ANY)] * 3 + [pl.BlockSpec(memory_space=pltpu.SMEM)],
        out_specs=pl.BlockSpec(memory_space=pltpu.VMEM),
        scratch_shapes=[
            pltpu.VMEM((stages, 2, STAGE, k), jnp.bfloat16),
            pltpu.VMEM((2, k, n), jnp.bfloat16),
            pltpu.VMEM((2, n, n), jnp.bfloat16),
            pltpu.VMEM((2, 2 * STAGE, n), jnp.float32),
            pltpu.VMEM((stages, owners, RB, LANES), jnp.bfloat16),
            pltpu.VMEM((stages, owners, RB, LANES), jnp.bfloat16),
            pltpu.VMEM((stages, others, RB, LANES), jnp.float32),
            pltpu.VMEM((stages, owners, RB, LANES), jnp.float32),
            dma, dma, dma((CUTS * stages,)), dma((CUTS * stages,)),
            dma((stages,)), dma((stages,)), dma((stages,)), dma((stages,)), dma((stages,)), dma((stages,)),
        ],
        compiler_params=pltpu.CompilerParams(
            collective_id=0, has_side_effects=True, vmem_limit_bytes=60 * 1024 * 1024
        ),
    )(stem, subtree, final_gates, group_rows)
    if out_rows == RB:
        return block
    return lax.dynamic_slice_in_dim(block, lax.axis_index(AXES) * out_rows % RB, out_rows, axis=0)


def solution(mesh):
    return jax.shard_map(
        local,
        mesh=mesh,
        in_specs=(
            P(AXES, None, None, None),
            P(AXES, None, None, None),
            P(),
            P(),
        ),
        out_specs=P(AXES, None),
        check_vma=False,
    )
```
